256 devices in a mesh: aux: 2 (over y_hi), blk: 128 (over z, y_lo, x, core).
Axes of the slice: x: 4, y: 4 (y_hi: 2, y_lo: 2; y = y_hi * 2 + y_lo), z: 8, core: 2. Of those that a mesh axis runs over, the one named last changes fastest.
Arguments:
- integrals: bfloat16 [8, 10240, 10240], P('aux', 'blk'), may hold values from -6 to 6
- coefficients: bfloat16 [10240, 256], P('blk'), may hold values from -0.0012207031 to 0.0012207031
Outputs:
- exchange_matrix: float32 [10240, 10240], P('blk', 'aux')
The draws below stay inside these ranges and needn't reach their ends.
All inputs are finite; a program needn't handle non-finite values.
Results may differ from the reference program's by a relative error of at most 0.0037.
Values may be sent and summed in bfloat16 or wider, within the bound.
No kernel may reach another device: no remote copies, remote signals or barrier semaphores. Data moves between devices by JAX's collectives and lax.ppermute only.
A program may use at most 128 MiB of HBM per device.

```python
import jax
import jax.numpy as jnp
from jax import lax

NAO = 10240
NOCC = 256
NAUX = 8


def block_levels(own_key, shape, split, low, high):
    level = 1.0
    for dim, blocks in split:
        draws = jax.random.uniform(jax.random.fold_in(jax.random.fold_in(own_key, 6), dim), (blocks,), jnp.float32, low / len(split), high / len(split))
        level = level * jnp.repeat(jnp.exp(draws), shape[dim] // blocks).reshape((-1,) + (1,) * (len(shape) - 1 - dim))
    return level


def gaussian(rng, extent, width, limit, pieces=(), held_as=jnp.bfloat16):
    entries = width * jax.random.normal(rng, extent, jnp.float32)
    if pieces:
        entries = entries * block_levels(rng, extent, pieces, -0.22, 0.18)
    return jnp.clip(entries, -limit, limit).astype(held_as)


def setup_inputs(seed: int = 0) -> dict:
    key_list = jax.random.split(jax.random.key(seed), 3)
    return {
        "integrals": gaussian(key_list[0], (NAUX, NAO, NAO), 1.0, 6.0, ((0, 2), (1, 128))),
        "coefficients": gaussian(key_list[1], (NAO, NOCC), (NAO * NAUX * NOCC) ** -0.5, 0.0012207031, ((0, 128),)),
    }


def reference(integrals, coefficients):
    def transform_block(block):
        return jnp.dot(block, coefficients, preferred_element_type=jnp.float32).astype(jnp.bfloat16)

    half_transformed = lax.map(transform_block, integrals)
    flattened = jnp.transpose(half_transformed, (1, 0, 2)).reshape(NAO, NAUX * NOCC)
    exchange_matrix = jnp.dot(flattened, flattened.T, preferred_element_type=jnp.float32)
    return exchange_matrix
```

```python
import jax
import jax.numpy as jnp
from jax import lax
from jax.sharding import Mesh, PartitionSpec as P

AXES = ("yh", "z", "yl", "x", "c")
SIZES = (2, 8, 2, 4, 2)
Y = ("yh", "yl")


def shift(value, axis, by):
    count = lax.axis_size(axis)
    return lax.ppermute(value, axis, [(i, (i + by) % count) for i in range(count)])


def ring8(value):
    up = down = value
    found = [(0, value)]
    for step in range(1, 4):
        up, down = shift(up, "z", 1), shift(down, "z", -1)
        found += [(-step, up), (step, down)]
    found.append((4, shift(up, "z", 1)))
    return found


def ring4(value, axis):
    half = value.shape[0] // 2
    up, down = shift(value, axis, 1), shift(value, axis, -1)
    far = [shift(up[:half], axis, 1), shift(down[half:], axis, -1)]
    return [(0, value), (-1, up), (1, down), (2, jnp.concatenate(far, 0))]


def placed(found, position, slot=lambda j: j):
    count = len(found)
    whole = jnp.zeros((count,) + found[0][1].shape, found[0][1].dtype)
    for offset, value in found:
        whole = lax.dynamic_update_index_in_dim(
            whole, value, slot((position + offset) % count), 0
        )
    return whole


def by_core(own, other, core):
    return jnp.where(core == 0, jnp.stack([own, other]), jnp.stack([other, own]))


def per_device(integrals, coefficients):
    aux, rows, basis = integrals.shape
    occ = coefficients.shape[1]
    half = occ // 2
    yh, yl = lax.axis_index("yh"), lax.axis_index("yl")
    z, x, c = lax.axis_index("z"), lax.axis_index("x"), lax.axis_index("c")

    own = lax.dynamic_slice_in_dim(coefficients, c * half, half, 1)
    given = lax.dynamic_slice_in_dim(coefficients, (1 - c) * half, half, 1)
    part = by_core(own, shift(given, "c", 1), c).reshape(2 * rows, half)
    along_z = placed(ring8(part), z)
    middle = along_z.shape[0] // 2
    other_y = jnp.concatenate(
        [shift(along_z[:middle], Y, 1), shift(along_z[middle:], Y, -1)], 0
    )
    along_y = jnp.where(yl == 0, jnp.stack([along_z, other_y]), jnp.stack([other_y, along_z]))
    along_x = placed(ring4(along_y, "x"), x)
    mine = along_x.transpose(2, 1, 0, 3, 4).reshape(basis, half)
    theirs = shift(mine, "c", 1)

    flat = integrals.reshape(aux * rows, basis)

    def transform(coefs):
        return jnp.dot(flat, coefs, preferred_element_type=jnp.float32).astype(jnp.bfloat16)

    pair = by_core(transform(mine), transform(theirs), c)
    unit = pair.reshape(2, aux, rows, half).transpose(2, 1, 0, 3).reshape(rows, aux * occ)

    at_y = placed([(0, unit), (-1, shift(unit, Y, 1)), (1, shift(unit, Y, -1)), (2, shift(unit, Y, 2))], yh * 2 + yl)
    at_x = placed(ring4(at_y, "x"), x)
    left = at_x.reshape(4, 2, 2, rows, aux * occ).transpose(2, 0, 3, 1, 4)
    left = left.reshape(8 * rows, 2 * aux * occ)

    moves = []
    for zi in range(8):
        home = zi // 4
        moves.append(((1 - home) * 8 + zi, home * 8 + 7 - zi))
    moved = lax.ppermute(unit, ("yh", "z"), moves)
    held = jnp.where(z // 4 == yh, unit, moved)

    def slot(j):
        return (j // 4) * 4 + jnp.where(j // 4 == yh, j % 4, 3 - j % 4)

    cols = placed(ring8(held), z, slot)
    cols = by_core(cols, shift(cols, "c", 1), c)
    right = cols.reshape(2, 2, 4, rows, aux * occ).transpose(2, 0, 3, 1, 4)
    right = right.reshape(8 * rows, 2 * aux * occ)

    block = lax.dot_general(left, right, (((1,), (1,)), ((), ())), preferred_element_type=jnp.float32)
    block = block.astype(jnp.bfloat16).reshape(8, rows, 8 * rows)
    pieces = lax.all_to_all(block, ("yl", "x"), split_axis=0, concat_axis=0, tiled=True)
    pieces = pieces.reshape(2, 4, rows, 4, 2, rows).transpose(2, 3, 0, 1, 4, 5)
    return pieces.reshape(rows, 64 * rows).astype(jnp.float32)


def solution(mesh):
    fine = Mesh(mesh.devices.reshape(SIZES), AXES)
    blk = ("z", "yl", "x", "c")
    return jax.shard_map(
        per_device,
        mesh=fine,
        in_specs=(P("yh", blk, None), P(blk, None)),
        out_specs=P(blk, "yh"),
        check_vma=False,
    )
```

```python
import jax
import jax.numpy as jnp
from jax import lax
from jax.experimental import pallas as pl
from jax.experimental.pallas import tpu as pltpu
from jax.sharding import Mesh, PartitionSpec as P

AXES = ("yh", "z", "yl", "x", "c")
SIZES = (2, 8, 2, 4, 2)
Y = ("yh", "yl")
ROWS, OCC, AUX, BASIS = 80, 256, 4, 10240
DEPTH = AUX * OCC
RING4 = (0, 3, 1, 2)
RING8 = (0, 7, 1, 6, 2, 5, 3, 4)
MIB = 1 << 20
VMEM = pl.BlockSpec(memory_space=pltpu.VMEM)
SMEM = pl.BlockSpec(memory_space=pltpu.SMEM)


def shift(value, axis, by):
    count = lax.axis_size(axis)
    return lax.ppermute(value, axis, [(i, (i + by) % count) for i in range(count)])


def swap(value):
    return shift(value, "c", 1)


def together(*values):
    return lax.optimization_barrier(values)


def call(kernel, outs, ins, mib, scratch=(), flops=0, moved=1):
    shapes = [jax.ShapeDtypeStruct(shape, jnp.bfloat16) for shape in outs]
    return pl.pallas_call(
        kernel,
        out_shape=shapes,
        in_specs=[spec for spec, _ in ins],
        out_specs=[VMEM] * len(shapes),
        scratch_shapes=list(scratch),
        compiler_params=pltpu.CompilerParams(vmem_limit_bytes=mib * MIB),
        cost_estimate=pl.CostEstimate(flops=flops, bytes_accessed=moved, transcendentals=0),
    )(*[value for _, value in ins])


def everywhere(value, axes):
    count = lax.axis_size(axes)
    copies = jnp.broadcast_to(value[None], (count,) + value.shape)
    return lax.all_to_all(copies, axes, split_axis=0, concat_axis=0, tiled=True)


def cut_kernel(first, second, *refs):
    low, high = refs[-2:]
    half = low.shape[0]
    low[...] = first[:half]
    high[...] = second[half:]


def cut(first, second, *also):
    half = (first.shape[0] // 2,) + first.shape[1:]
    return call(cut_kernel, [half, half], [(VMEM, v) for v in (first, second, *also)], 4)


def transform_kernel(where, integrals, *refs):
    pieces, (out, coefs) = refs[:-2], refs[-2:]
    yl, x, c = where[1], where[3], where[4]

    def keep(ref, core, other_y, along_x, first):
        low = 1 - yl if other_y else yl
        at_x = lax.rem(x + along_x + 4, 4)
        for i in range(ref.shape[0]):
            coefs[first + i, (low * 4 + at_x) * 2 + core] = ref[i]

    count = len(pieces) // 2
    for other in range(2):
        core = 1 - c if other else c
        near, left, right, far0, far1, ynear0, ynear1, yleft, yright, yfar0, yfar1 = pieces[other * count:(other + 1) * count]
        for ref, other_y, at_x, first in (
            (near, 0, 0, 0), (left, 0, -1, 0), (right, 0, 1, 0), (far0, 0, 2, 0), (far1, 0, 2, 4),
            (ynear0, 1, 0, 0), (ynear1, 1, 0, 4), (yleft, 1, -1, 0), (yright, 1, 1, 0), (yfar0, 1, 2, 0), (yfar1, 1, 2, 4),
        ):
            keep(ref, core, other_y, at_x, first)

    total = jnp.zeros((AUX * ROWS, OCC), jnp.float32)
    for z in range(8):
        chunk = coefs[z].reshape(1280, OCC)
        total += jnp.dot(integrals[:, z * 1280:(z + 1) * 1280], chunk, preferred_element_type=jnp.float32)
    half = total.astype(jnp.bfloat16)
    for p in range(AUX):
        out[:, p * OCC:(p + 1) * OCC] = half[p * ROWS:(p + 1) * ROWS]


def transform(where, flat, pieces):
    return call(
        transform_kernel,
        [(ROWS, DEPTH)],
        [(SMEM, where), (VMEM, flat)] + [(VMEM, p) for p in pieces],
        16,
        [pltpu.VMEM((8, 16, ROWS, OCC), jnp.bfloat16)],
        2 * 320 * BASIS * OCC, 12 * MIB,
    )[0]


def held_kernel(where, unit, moved, out):
    home = where[0] == where[2] // 4

    @pl.when(home)
    def _():
        out[...] = unit[...]

    @pl.when(jnp.logical_not(home))
    def _():
        out[...] = moved[...]


def stack_kernel(*refs):
    for i, ref in enumerate(refs[:-1]):
        refs[-1][i] = ref[...]


def stack(*values):
    return call(stack_kernel, [(len(values),) + values[0].shape], [(VMEM, v) for v in values], 4)[0]


def product_kernel(where, near, left, right, far0, far1, *refs):
    cols, (out, lefts, rights) = refs[:16], refs[16:]
    yh, yl, z, x, c = (where[i] for i in range(5))
    for ref, along_x, first in ((near, 0, 0), (left, 3, 0), (right, 1, 0), (far0, 2, 0), (far1, 2, 2)):
        at_x = lax.rem(x + along_x, 4)
        for i in range(ref.shape[0]):
            at_y = lax.rem(yh * 2 + yl + RING4[first + i], 4)
            lefts[at_y // 2, (at_y % 2) * 4 + at_x] = ref[i]
    for other in range(2):
        core = 1 - c if other else c
        for ref, along in zip(cols[other * 8:other * 8 + 8], RING8):
            at_z = lax.rem(z + along, 8)
            side = at_z // 4
            q = jnp.where(side == yh, at_z % 4, 3 - at_z % 4)
            rights[side, q * 2 + core] = ref[...]
    total = None
    for side in range(2):
        part = lax.dot_general(
            lefts[side].reshape(640, DEPTH), rights[side].reshape(640, DEPTH),
            (((1,), (1,)), ((), ())), preferred_element_type=jnp.float32,
        )
        total = part if total is None else total + part
    out[...] = total.astype(jnp.bfloat16).reshape(8, ROWS, 640)


def product(where, rows, cols):
    return call(
        product_kernel,
        [(8, ROWS, 640)],
        [(SMEM, where)] + [(VMEM, v) for v in rows + cols],
        16,
        [pltpu.VMEM((2, 8, ROWS, DEPTH), jnp.bfloat16)] * 2,
        2 * 640 * 640 * 2 * DEPTH, 6 * MIB,
    )[0]


def spread_kernel(pieces, out):
    for q in range(4):
        for s in range(8):
            at = q * 1280 + s * 160
            out[:, at:at + 160] = pieces[s, :, q * 160:(q + 1) * 160].astype(jnp.float32)


def spread(pieces):
    return pl.pallas_call(
        spread_kernel,
        out_shape=jax.ShapeDtypeStruct((ROWS, 5120), jnp.float32),
        in_specs=[VMEM],
        out_specs=VMEM,
        compiler_params=pltpu.CompilerParams(vmem_limit_bytes=8 * MIB),
        cost_estimate=pl.CostEstimate(flops=0, bytes_accessed=4 * MIB, transcendentals=0),
    )(pieces)


def gather_coefficients(own, flat):
    near = everywhere(own, "z")
    low, high = cut(near, near, flat)
    left, right = shift(near, "x", 1), shift(near, "x", -1)
    ynear = shift(low, Y, 1), shift(high, Y, -1)
    left, right = together(left, right)
    far = cut(left, right)
    far = shift(far[0], "x", 1), shift(far[1], "x", -1)
    yleft, yright = shift(left, Y, 1), shift(right, Y, -1)
    *far, yleft, yright = together(*far, yleft, yright)
    yfar = together(shift(far[0], Y, 1), shift(far[1], Y, -1))
    return [near, left, right, *far, *ynear, yleft, yright, *yfar]


def per_device(integrals, coefficients):
    where = jnp.stack([lax.axis_index(a) for a in ("yh", "yl", "z", "x", "c")]).astype(jnp.int32)
    where, coefficients = together(where, coefficients)
    flat = integrals.reshape(AUX * ROWS, BASIS)

    pieces = gather_coefficients(coefficients, flat)
    pieces += [swap(p) for p in pieces]
    unit = transform(where, flat, pieces)

    moves = []
    for zi in range(8):
        home = zi // 4
        moves.append(((1 - home) * 8 + zi, home * 8 + 7 - zi))
    moved = lax.ppermute(unit, ("yh", "z"), moves)
    at_y = stack(unit, shift(unit, Y, 1), shift(unit, Y, -1), shift(unit, Y, 2))
    held = call(held_kernel, [unit.shape], [(SMEM, where), (VMEM, unit), (VMEM, moved)], 4)[0]

    up, down = shift(held, "z", 1), shift(held, "z", -1)
    up, down, at_y = together(up, down, at_y)
    left, right = shift(at_y, "x", 1), shift(at_y, "x", -1)
    up2, down2 = shift(up, "z", 1), shift(down, "z", -1)
    up3, down3 = shift(up2, "z", 1), shift(down2, "z", -1)
    up3, down3, left, right = together(up3, down3, left, right)
    far = cut(left, right)
    far = [shift(far[0], "x", 1), shift(far[1], "x", -1)]
    up4 = shift(up3, "z", 1)
    up4, *far = together(up4, *far)
    cols = [held, up, down, up2, down2, up3, down3, up4]
    cols += [swap(v) for v in cols]

    block = product(where, [at_y, left, right, *far], cols)
    return spread(lax.all_to_all(block, ("yl", "x"), split_axis=0, concat_axis=0, tiled=True))


def solution(mesh):
    fine = Mesh(mesh.devices.reshape(SIZES), AXES)
    blk = ("z", "yl", "x", "c")
    return jax.shard_map(
        per_device,
        mesh=fine,
        in_specs=(P("yh", blk, None), P(blk, None)),
        out_specs=P(blk, "yh"),
        check_vma=False,
    )
```

```python
import jax
import jax.numpy as jnp
from jax import lax
from jax.experimental import pallas as pl
from jax.experimental.pallas import tpu as pltpu
from jax.sharding import Mesh, PartitionSpec as P

AXES = ("yh", "z", "yl", "x", "c")
SIZES = (2, 8, 2, 4, 2)
Y = ("yh", "yl")
ROWS, OCC, AUX, BASIS = 80, 256, 4, 10240
DEPTH = AUX * OCC
RING8 = (0, 7, 1, 6, 2, 5, 3, 4)
MIB = 1 << 20
VMEM = pl.BlockSpec(memory_space=pltpu.VMEM)
SMEM = pl.BlockSpec(memory_space=pltpu.SMEM)


def shift(value, axis, by):
    count = lax.axis_size(axis)
    return lax.ppermute(value, axis, [(i, (i + by) % count) for i in range(count)])


def swap(value):
    return shift(value, "c", 1)


def together(*values):
    return lax.optimization_barrier(values)


def call(kernel, outs, ins, mib, scratch=(), flops=0, moved=1):
    shapes = [jax.ShapeDtypeStruct(shape, jnp.bfloat16) for shape in outs]
    return pl.pallas_call(
        kernel,
        out_shape=shapes,
        in_specs=[spec for spec, _ in ins],
        out_specs=[VMEM] * len(shapes),
        scratch_shapes=list(scratch),
        compiler_params=pltpu.CompilerParams(vmem_limit_bytes=mib * MIB),
        cost_estimate=pl.CostEstimate(flops=flops, bytes_accessed=moved, transcendentals=0),
    )(*[value for _, value in ins])


def everywhere(value, axes):
    count = lax.axis_size(axes)
    copies = jnp.broadcast_to(value[None], (count,) + value.shape)
    return lax.all_to_all(copies, axes, split_axis=0, concat_axis=0, tiled=True)


def cut_kernel(first, second, *refs):
    low, high = refs[-2:]
    half = low.shape[0]
    low[...] = first[:half]
    high[...] = second[half:]


def cut(first, second, *also):
    half = (first.shape[0] // 2,) + first.shape[1:]
    return call(cut_kernel, [half, half], [(VMEM, v) for v in (first, second, *also)], 4)


def transform_kernel(where, integrals, *refs):
    pieces, (out, coefs) = refs[:-2], refs[-2:]
    yl, x, c = where[1], where[3], where[4]

    def keep(ref, core, other_y, along_x, first):
        low = 1 - yl if other_y else yl
        at_x = lax.rem(x + along_x + 4, 4)
        for i in range(ref.shape[0]):
            coefs[first + i, (low * 4 + at_x) * 2 + core] = ref[i]

    count = len(pieces) // 2
    for other in range(2):
        core = 1 - c if other else c
        near, left, right, far0, far1, ynear0, ynear1, yleft, yright, yfar0, yfar1 = pieces[other * count:(other + 1) * count]
        for ref, other_y, at_x, first in (
            (near, 0, 0, 0), (left, 0, -1, 0), (right, 0, 1, 0), (far0, 0, 2, 0), (far1, 0, 2, 4),
            (ynear0, 1, 0, 0), (ynear1, 1, 0, 4), (yleft, 1, -1, 0), (yright, 1, 1, 0), (yfar0, 1, 2, 0), (yfar1, 1, 2, 4),
        ):
            keep(ref, core, other_y, at_x, first)

    total = jnp.zeros((AUX * ROWS, OCC), jnp.float32)
    for z in range(8):
        chunk = coefs[z].reshape(1280, OCC)
        total += jnp.dot(integrals[:, z * 1280:(z + 1) * 1280], chunk, preferred_element_type=jnp.float32)
    half = total.astype(jnp.bfloat16)
    for p in range(AUX):
        out[:, p * OCC:(p + 1) * OCC] = half[p * ROWS:(p + 1) * ROWS]


def transform(where, flat, pieces):
    return call(
        transform_kernel,
        [(ROWS, DEPTH)],
        [(SMEM, where), (VMEM, flat)] + [(VMEM, p) for p in pieces],
        16,
        [pltpu.VMEM((8, 16, ROWS, OCC), jnp.bfloat16)],
        2 * 320 * BASIS * OCC, 12 * MIB,
    )[0]


def stack_kernel(*refs):
    for i, ref in enumerate(refs[:-1]):
        refs[-1][i] = ref[...]


def stack(*values):
    return call(stack_kernel, [(len(values),) + values[0].shape], [(VMEM, v) for v in values], 4)[0]


def product_kernel(where, near, left, right, far0, far1, *refs):
    cols, (out, lefts, rights) = refs[:16], refs[16:]
    yl, z, x, c = (where[i] for i in range(1, 5))
    for ref, along_x, first in ((near, 0, 0), (left, 3, 0), (right, 1, 0), (far0, 2, 0), (far1, 2, 1)):
        for i in range(ref.shape[0]):
            side = 1 - yl if first + i else yl
            lefts[side * 4 + lax.rem(x + along_x, 4)] = ref[i]
    for other in range(2):
        core = 1 - c if other else c
        for ref, along in zip(cols[other * 8:other * 8 + 8], RING8):
            rights[lax.rem(z + along, 8), core] = ref[...]
    block = lax.dot_general(
        lefts[...].reshape(640, DEPTH), rights[...].reshape(1280, DEPTH),
        (((1,), (1,)), ((), ())), preferred_element_type=jnp.float32,
    ).astype(jnp.bfloat16)
    for h in range(2):
        out[h * 8:(h + 1) * 8] = block[:, h * 640:(h + 1) * 640].reshape(8, ROWS, 640)


def product(where, rows, cols):
    return call(
        product_kernel,
        [(16, ROWS, 640)],
        [(SMEM, where)] + [(VMEM, v) for v in rows + cols],
        20,
        [
            pltpu.VMEM((8, ROWS, DEPTH), jnp.bfloat16),
            pltpu.VMEM((8, 2, ROWS, DEPTH), jnp.bfloat16),
        ],
        2 * 640 * 1280 * DEPTH, 6 * MIB,
    )[0]


def spread_kernel(pieces, out):
    for q in range(4):
        for s in range(8):
            at = q * 1280 + s * 160
            lanes = slice(q * 160, (q + 1) * 160)
            out[:, at:at + 160] = pieces[s, :, lanes].astype(jnp.float32) + pieces[8 + s, :, lanes].astype(jnp.float32)


def spread(pieces):
    return pl.pallas_call(
        spread_kernel,
        out_shape=jax.ShapeDtypeStruct((ROWS, 5120), jnp.float32),
        in_specs=[VMEM],
        out_specs=VMEM,
        compiler_params=pltpu.CompilerParams(vmem_limit_bytes=8 * MIB),
        cost_estimate=pl.CostEstimate(flops=0, bytes_accessed=4 * MIB, transcendentals=0),
    )(pieces)


def gather_coefficients(own, flat):
    near = everywhere(own, "z")
    low, high = cut(near, near, flat)
    left, right = shift(near, "x", 1), shift(near, "x", -1)
    ynear = shift(low, Y, 1), shift(high, Y, -1)
    left, right = together(left, right)
    far = cut(left, right)
    far = shift(far[0], "x", 1), shift(far[1], "x", -1)
    yleft, yright = shift(left, Y, 1), shift(right, Y, -1)
    *far, yleft, yright = together(*far, yleft, yright)
    yfar = together(shift(far[0], Y, 1), shift(far[1], Y, -1))
    return [near, left, right, *far, *ynear, yleft, yright, *yfar]


def per_device(integrals, coefficients):
    where = jnp.stack([lax.axis_index(a) for a in ("yh", "yl", "z", "x", "c")]).astype(jnp.int32)
    where, coefficients = together(where, coefficients)
    flat = integrals.reshape(AUX * ROWS, BASIS)

    pieces = gather_coefficients(coefficients, flat)
    pieces += [swap(p) for p in pieces]
    unit = transform(where, flat, pieces)

    ynear = shift(unit, "yl", 1)
    up, down = shift(unit, "z", 1), shift(unit, "z", -1)
    near = stack(unit, ynear)
    left, right = shift(near, "x", 1), shift(near, "x", -1)
    up2, down2 = shift(up, "z", 1), shift(down, "z", -1)
    up3, down3 = shift(up2, "z", 1), shift(down2, "z", -1)
    up3, down3, left, right = together(up3, down3, left, right)
    far = cut(left, right)
    far = [shift(far[0], "x", 1), shift(far[1], "x", -1)]
    up4 = shift(up3, "z", 1)
    up4, *far = together(up4, *far)
    cols = [unit, up, down, up2, down2, up3, down3, up4]
    cols += [swap(v) for v in cols]

    block = product(where, [near, left, right, *far], cols)
    return spread(lax.all_to_all(block, ("yh", "yl", "x"), split_axis=0, concat_axis=0, tiled=True))


def solution(mesh):
    fine = Mesh(mesh.devices.reshape(SIZES), AXES)
    blk = ("z", "yl", "x", "c")
    return jax.shard_map(
        per_device,
        mesh=fine,
        in_specs=(P("yh", blk, None), P(blk, None)),
        out_specs=P(blk, "yh"),
        check_vma=False,
    )
```

```python
import jax
import jax.numpy as jnp
from jax import lax
from jax.experimental import pallas as pl
from jax.experimental.pallas import tpu as pltpu
from jax.sharding import Mesh, PartitionSpec as P

AXES = ("yh", "z", "yl", "x", "c")
SIZES = (2, 8, 2, 4, 2)
Y = ("yh", "yl")
ROWS, OCC, AUX, BASIS = 80, 256, 4, 10240
DEPTH = AUX * OCC
RING8 = (0, 7, 1, 6, 2, 5, 3, 4)
MIB = 1 << 20
VMEM = pl.BlockSpec(memory_space=pltpu.VMEM)
SMEM = pl.BlockSpec(memory_space=pltpu.SMEM)


def shift(value, axis, by):
    count = lax.axis_size(axis)
    return lax.ppermute(value, axis, [(i, (i + by) % count) for i in range(count)])


def swap(value):
    return shift(value, "c", 1)


def cross(value):
    steps = [(zi * 2 + ci, (zi - 1) % 8 * 2 + 1 - ci) for zi in range(8) for ci in range(2)]
    return lax.ppermute(value, ("z", "c"), steps)


def together(*values):
    return lax.optimization_barrier(values)


def call(kernel, outs, ins, mib, scratch=(), flops=0, moved=1):
    shapes = [jax.ShapeDtypeStruct(shape, jnp.bfloat16) for shape in outs]
    return pl.pallas_call(
        kernel,
        out_shape=shapes,
        in_specs=[spec for spec, _ in ins],
        out_specs=[VMEM] * len(shapes),
        scratch_shapes=list(scratch),
        compiler_params=pltpu.CompilerParams(vmem_limit_bytes=mib * MIB),
        cost_estimate=pl.CostEstimate(flops=flops, bytes_accessed=moved, transcendentals=0),
    )(*[value for _, value in ins])


def everywhere(value, axes):
    count = lax.axis_size(axes)
    copies = jnp.broadcast_to(value[None], (count,) + value.shape)
    return lax.all_to_all(copies, axes, split_axis=0, concat_axis=0, tiled=True)


def cut_kernel(first, second, *refs):
    low, high = refs[-2:]
    half = low.shape[0]
    low[...] = first[:half]
    high[...] = second[half:]


def cut(first, second, *also):
    half = (first.shape[0] // 2,) + first.shape[1:]
    return call(cut_kernel, [half, half], [(VMEM, v) for v in (first, second, *also)], 4)


def transform_kernel(where, integrals, *refs):
    pieces, (out, coefs) = refs[:-2], refs[-2:]
    yl, x, c = where[1], where[3], where[4]

    def keep(ref, core, other_y, along_x, first):
        low = 1 - yl if other_y else yl
        at_x = lax.rem(x + along_x + 4, 4)
        for i in range(ref.shape[0]):
            coefs[first + i, (low * 4 + at_x) * 2 + core] = ref[i]

    count = len(pieces) // 2
    for other in range(2):
        core = 1 - c if other else c
        near, left, right, far0, far1, ynear0, ynear1, yleft, yright, yfar0, yfar1 = pieces[other * count:(other + 1) * count]
        for ref, other_y, at_x, first in (
            (near, 0, 0, 0), (left, 0, -1, 0), (right, 0, 1, 0), (far0, 0, 2, 0), (far1, 0, 2, 4),
            (ynear0, 1, 0, 0), (ynear1, 1, 0, 4), (yleft, 1, -1, 0), (yright, 1, 1, 0), (yfar0, 1, 2, 0), (yfar1, 1, 2, 4),
        ):
            keep(ref, core, other_y, at_x, first)

    total = jnp.zeros((AUX * ROWS, OCC), jnp.float32)
    for z in range(8):
        chunk = coefs[z].reshape(1280, OCC)
        total += jnp.dot(integrals[:, z * 1280:(z + 1) * 1280], chunk, preferred_element_type=jnp.float32)
    half = total.astype(jnp.bfloat16)
    for p in range(AUX):
        out[:, p * OCC:(p + 1) * OCC] = half[p * ROWS:(p + 1) * ROWS]


def transform(where, flat, pieces):
    return call(
        transform_kernel,
        [(ROWS, DEPTH)],
        [(SMEM, where), (VMEM, flat)] + [(VMEM, p) for p in pieces],
        16,
        [pltpu.VMEM((8, 16, ROWS, OCC), jnp.bfloat16)],
        2 * 320 * BASIS * OCC, 12 * MIB,
    )[0]


def stack_kernel(*refs):
    for i, ref in enumerate(refs[:-1]):
        refs[-1][i] = ref[...]


def stack(*values):
    return call(stack_kernel, [(len(values),) + values[0].shape], [(VMEM, v) for v in values], 4)[0]


def product_kernel(where, near, left, right, far, yfar, *refs):
    cols, (out, lefts, rights) = refs[:16], refs[16:]
    yl, z, x, c = (where[i] for i in range(1, 5))
    for ref, along_x in ((near, 0), (left, 3), (right, 1)):
        for i in range(2):
            side = 1 - yl if i else yl
            lefts[side * 4 + lax.rem(x + along_x, 4)] = ref[i]
    lefts[yl * 4 + lax.rem(x + 2, 4)] = far[...]
    lefts[(1 - yl) * 4 + lax.rem(x + 2, 4)] = yfar[...]
    for other in range(2):
        core = 1 - c if other else c
        for ref, along in zip(cols[other * 8:other * 8 + 8], RING8):
            rights[lax.rem(z + along, 8), core] = ref[...]
    block = lax.dot_general(
        lefts[...].reshape(640, DEPTH), rights[...].reshape(1280, DEPTH),
        (((1,), (1,)), ((), ())), preferred_element_type=jnp.float32,
    ).astype(jnp.bfloat16)
    for h in range(2):
        out[h * 8:(h + 1) * 8] = block[:, h * 640:(h + 1) * 640].reshape(8, ROWS, 640)


def product(where, rows, cols):
    return call(
        product_kernel,
        [(16, ROWS, 640)],
        [(SMEM, where)] + [(VMEM, v) for v in rows + cols],
        20,
        [
            pltpu.VMEM((8, ROWS, DEPTH), jnp.bfloat16),
            pltpu.VMEM((8, 2, ROWS, DEPTH), jnp.bfloat16),
        ],
        2 * 640 * 1280 * DEPTH, 6 * MIB,
    )[0]


def spread_kernel(pieces, out):
    for q in range(4):
        for s in range(8):
            at = q * 1280 + s * 160
            lanes = slice(q * 160, (q + 1) * 160)
            out[:, at:at + 160] = pieces[s, :, lanes].astype(jnp.float32) + pieces[8 + s, :, lanes].astype(jnp.float32)


def spread(pieces):
    return pl.pallas_call(
        spread_kernel,
        out_shape=jax.ShapeDtypeStruct((ROWS, 5120), jnp.float32),
        in_specs=[VMEM],
        out_specs=VMEM,
        compiler_params=pltpu.CompilerParams(vmem_limit_bytes=8 * MIB),
        cost_estimate=pl.CostEstimate(flops=0, bytes_accessed=4 * MIB, transcendentals=0),
    )(pieces)


def gather_coefficients(own, flat):
    near = everywhere(own, "z")
    low, high = cut(near, near, flat)
    left, right = shift(near, "x", 1), shift(near, "x", -1)
    ynear = shift(low, Y, 1), shift(high, Y, -1)
    left, right = together(left, right)
    far = cut(left, right)
    far = shift(far[0], "x", 1), shift(far[1], "x", -1)
    yleft, yright = shift(left, Y, 1), shift(right, Y, -1)
    *far, yleft, yright = together(*far, yleft, yright)
    yfar = together(shift(far[0], Y, 1), shift(far[1], Y, -1))
    return [near, left, right, *far, *ynear, yleft, yright, *yfar]


def per_device(integrals, coefficients):
    where = jnp.stack([lax.axis_index(a) for a in ("yh", "yl", "z", "x", "c")]).astype(jnp.int32)
    where, coefficients = together(where, coefficients)
    flat = integrals.reshape(AUX * ROWS, BASIS)

    pieces = gather_coefficients(coefficients, flat)
    pieces += [swap(p) for p in pieces]
    unit = transform(where, flat, pieces)

    ynear = shift(unit, "yl", 1)
    up, down = shift(unit, "z", 1), shift(unit, "z", -1)
    near = stack(unit, ynear)
    left, right = shift(near, "x", 1), shift(near, "x", -1)
    far = shift(unit, "x", 2)
    yfar = shift(far, "yl", 1)
    up2, down2 = shift(up, "z", 1), shift(down, "z", -1)
    up3, down3 = shift(up2, "z", 1), shift(down2, "z", -1)
    up3, down3, left, right, far, yfar = together(up3, down3, left, right, far, yfar)
    cols = [unit, up, down, up2, down2, up3, down3]
    cols += [shift(up3, "z", 1), *(swap(v) for v in cols), cross(down3)]

    block = product(where, [near, left, right, far, yfar], cols)
    return spread(lax.all_to_all(block, ("yh", "yl", "x"), split_axis=0, concat_axis=0, tiled=True))


def solution(mesh):
    fine = Mesh(mesh.devices.reshape(SIZES), AXES)
    blk = ("z", "yl", "x", "c")
    return jax.shard_map(
        per_device,
        mesh=fine,
        in_specs=(P("yh", blk, None), P(blk, None)),
        out_specs=P(blk, "yh"),
        check_vma=False,
    )
```

```python
import jax
import jax.numpy as jnp
from jax import lax
from jax.experimental import pallas as pl
from jax.experimental.pallas import tpu as pltpu
from jax.sharding import Mesh, PartitionSpec as P

AXES = ("yh", "z", "yl", "x", "c")
SIZES = (2, 8, 2, 4, 2)
Y = ("yh", "yl")
ROWS, OCC, AUX, BASIS = 80, 256, 4, 10240
DEPTH = AUX * OCC
RING8 = (0, 7, 1, 6, 2, 5, 3, 4)
MIB = 1 << 20
VMEM = pl.BlockSpec(memory_space=pltpu.VMEM)
SMEM = pl.BlockSpec(memory_space=pltpu.SMEM)


def shift(value, axis, by):
    count = lax.axis_size(axis)
    return lax.ppermute(value, axis, [(i, (i + by) % count) for i in range(count)])


def swap(value):
    return shift(value, "c", 1)


def cross(value):
    steps = [(zi * 2 + ci, (zi - 1) % 8 * 2 + 1 - ci) for zi in range(8) for ci in range(2)]
    return lax.ppermute(value, ("z", "c"), steps)


def together(*values):
    return lax.optimization_barrier(values)


def call(kernel, outs, ins, mib, scratch=(), flops=0, moved=1):
    shapes = [jax.ShapeDtypeStruct(shape, jnp.bfloat16) for shape in outs]
    return pl.pallas_call(
        kernel,
        out_shape=shapes,
        in_specs=[spec for spec, _ in ins],
        out_specs=[VMEM] * len(shapes),
        scratch_shapes=list(scratch),
        compiler_params=pltpu.CompilerParams(vmem_limit_bytes=mib * MIB),
        cost_estimate=pl.CostEstimate(flops=flops, bytes_accessed=moved, transcendentals=0),
    )(*[value for _, value in ins])


def everywhere(value, axes):
    count = lax.axis_size(axes)
    copies = jnp.broadcast_to(value[None], (count,) + value.shape)
    return lax.all_to_all(copies, axes, split_axis=0, concat_axis=0, tiled=True)


def cut_kernel(first, second, *refs):
    low, high = refs[-2:]
    half = low.shape[0]
    low[...] = first[:half]
    high[...] = second[half:]


def cut(first, second, *also):
    half = (first.shape[0] // 2,) + first.shape[1:]
    return call(cut_kernel, [half, half], [(VMEM, v) for v in (first, second, *also)], 4)


def transform_kernel(where, integrals, *refs):
    pieces, (out, coefs) = refs[:-2], refs[-2:]
    yl, x, c = where[1], where[3], where[4]

    def keep(ref, core, other_y, along_x, first):
        low = 1 - yl if other_y else yl
        at_x = lax.rem(x + along_x + 4, 4)
        for i in range(ref.shape[0]):
            coefs[first + i, (low * 4 + at_x) * 2 + core] = ref[i]

    count = len(pieces) // 2
    for other in range(2):
        core = 1 - c if other else c
        near, left, right, far0, far1, ynear0, ynear1, yleft, yright, yfar0, yfar1 = pieces[other * count:(other + 1) * count]
        for ref, other_y, at_x, first in (
            (near, 0, 0, 0), (left, 0, -1, 0), (right, 0, 1, 0), (far0, 0, 2, 0), (far1, 0, 2, 4),
            (ynear0, 1, 0, 0), (ynear1, 1, 0, 4), (yleft, 1, -1, 0), (yright, 1, 1, 0), (yfar0, 1, 2, 0), (yfar1, 1, 2, 4),
        ):
            keep(ref, core, other_y, at_x, first)

    total = jnp.zeros((AUX * ROWS, OCC), jnp.float32)
    for z in range(8):
        chunk = coefs[z].reshape(1280, OCC)
        total += jnp.dot(integrals[:, z * 1280:(z + 1) * 1280], chunk, preferred_element_type=jnp.float32)
    half = total.astype(jnp.bfloat16)
    for p in range(AUX):
        out[:, p * OCC:(p + 1) * OCC] = half[p * ROWS:(p + 1) * ROWS]


def transform(where, flat, pieces):
    return call(
        transform_kernel,
        [(ROWS, DEPTH)],
        [(SMEM, where), (VMEM, flat)] + [(VMEM, p) for p in pieces],
        16,
        [pltpu.VMEM((8, 16, ROWS, OCC), jnp.bfloat16)],
        2 * 320 * BASIS * OCC, 12 * MIB,
    )[0]


def stack_kernel(*refs):
    for i, ref in enumerate(refs[:-1]):
        refs[-1][i] = ref[...]


def stack(*values):
    return call(stack_kernel, [(len(values),) + values[0].shape], [(VMEM, v) for v in values], 4)[0]


def product_kernel(where, near, left, right, far, yfar, *refs):
    cols, (out, lefts, rights) = refs[:16], refs[16:]
    yl, z, x, c = (where[i] for i in range(1, 5))
    for ref, along_x in ((near, 0), (left, 3), (right, 1)):
        for i in range(2):
            side = 1 - yl if i else yl
            lefts[side * 4 + lax.rem(x + along_x, 4)] = ref[i]
    lefts[yl * 4 + lax.rem(x + 2, 4)] = far[...]
    lefts[(1 - yl) * 4 + lax.rem(x + 2, 4)] = yfar[...]
    for other in range(2):
        core = 1 - c if other else c
        for ref, along in zip(cols[other * 8:other * 8 + 8], RING8):
            rights[lax.rem(z + along, 8), core] = ref[...]
    block = lax.dot_general(
        lefts[...].reshape(640, DEPTH), rights[...].reshape(1280, DEPTH),
        (((1,), (1,)), ((), ())), preferred_element_type=jnp.float32,
    ).astype(jnp.bfloat16)
    for h in range(2):
        out[h * 8:(h + 1) * 8] = block[:, h * 640:(h + 1) * 640].reshape(8, ROWS, 640)


def product(where, rows, cols):
    return call(
        product_kernel,
        [(16, ROWS, 640)],
        [(SMEM, where)] + [(VMEM, v) for v in rows + cols],
        20,
        [
            pltpu.VMEM((8, ROWS, DEPTH), jnp.bfloat16),
            pltpu.VMEM((8, 2, ROWS, DEPTH), jnp.bfloat16),
        ],
        2 * 640 * 1280 * DEPTH, 6 * MIB,
    )[0]


def spread_kernel(pieces, out):
    for q in range(4):
        for s in range(8):
            at = q * 1280 + s * 160
            lanes = slice(q * 160, (q + 1) * 160)
            out[:, at:at + 160] = pieces[s, :, lanes].astype(jnp.float32) + pieces[8 + s, :, lanes].astype(jnp.float32)


def spread(pieces):
    return pl.pallas_call(
        spread_kernel,
        out_shape=jax.ShapeDtypeStruct((ROWS, 5120), jnp.float32),
        in_specs=[VMEM],
        out_specs=VMEM,
        compiler_params=pltpu.CompilerParams(vmem_limit_bytes=8 * MIB),
        cost_estimate=pl.CostEstimate(flops=0, bytes_accessed=4 * MIB, transcendentals=0),
    )(pieces)


def gather_coefficients(own, flat):
    near = everywhere(own, "z")
    low, high = cut(near, near, flat)
    left, right = shift(near, "x", 1), shift(near, "x", -1)
    ynear = shift(low, Y, 1), shift(high, Y, -1)
    left, right = together(left, right)
    far = shift(low, "x", 2), shift(high, "x", 2)
    yleft, yright = shift(left, Y, 1), shift(right, Y, -1)
    *far, yleft, yright = together(*far, yleft, yright)
    yfar = together(shift(far[0], Y, 1), shift(far[1], Y, -1))
    return [near, left, right, *far, *ynear, yleft, yright, *yfar]


def per_device(integrals, coefficients):
    where = jnp.stack([lax.axis_index(a) for a in ("yh", "yl", "z", "x", "c")]).astype(jnp.int32)
    where, coefficients = together(where, coefficients)
    flat = integrals.reshape(AUX * ROWS, BASIS)

    pieces = gather_coefficients(coefficients, flat)
    pieces += [swap(p) for p in pieces]
    unit = transform(where, flat, pieces)

    ynear = shift(unit, "yl", 1)
    up, down = shift(unit, "z", 1), shift(unit, "z", -1)
    near = stack(unit, ynear)
    left, right = shift(near, "x", 1), shift(near, "x", -1)
    far = shift(unit, "x", 2)
    yfar = shift(far, "yl", 1)
    up2, down2 = shift(up, "z", 1), shift(down, "z", -1)
    up3, down3 = shift(up2, "z", 1), shift(down2, "z", -1)
    up3, down3, left, right, far, yfar = together(up3, down3, left, right, far, yfar)
    cols = [unit, up, down, up2, down2, up3, down3]
    cols += [shift(up3, "z", 1), *(swap(v) for v in cols), cross(down3)]

    block = product(where, [near, left, right, far, yfar], cols)
    return spread(lax.all_to_all(block, ("yh", "yl", "x"), split_axis=0, concat_axis=0, tiled=True))


def solution(mesh):
    fine = Mesh(mesh.devices.reshape(SIZES), AXES)
    blk = ("z", "yl", "x", "c")
    return jax.shard_map(
        per_device,
        mesh=fine,
        in_specs=(P("yh", blk, None), P(blk, None)),
        out_specs=P(blk, "yh"),
        check_vma=False,
    )
```
